32 devices in a mesh: mol: 2 (over y), pair: 8 (over z, core), int: 2 (over x), rep: 1.
Axes of the slice: x: 2, y: 2, z: 4, core: 2. Of those that a mesh axis runs over, the one named last changes fastest.
Arguments:
- amplitudes: bfloat16 [64, 4, 32, 4096], P(('mol', 'pair'), None, ('int', 'rep')), parts along dimension 0, may hold values from -6 to 6
- amp_tiles: int32 [64, 4], P(('mol', 'pair')), parts along dimension 0, may hold values from 0 to 7, all different within a row; in each aligned block of 4 rows (0 to 3, 4 to 7, ...) at most 2 rows name the same one
- integrals: bfloat16 [16, 4096, 2, 4096], P(('mol', 'pair'), None, None, ('int', 'rep')), parts along dimension 0, may hold values from -0.09375 to 0.09375
- int_tiles: int32 [16, 2], P('mol'), parts along dimension 0, may hold values from 0 to 7, all different within a row
- occupied_energy: float32 [64, 32], P(('mol', 'pair')), parts along dimension 0, may hold values from -3 to -0.5
- virtual_energy: float32 [16, 4096], P('mol', ('int', 'rep')), parts along dimension 0, may hold values from 0.5 to 6
Outputs:
- amplitude_step: bfloat16 [64, 8, 32, 4096], P(('mol', 'pair'), None, None, ('int', 'rep')), parts along dimension 0
The draws below stay inside these ranges and needn't reach their ends.
There are 2 independent parts, one for each index of `mol`. The reference program is written for one: setup_inputs(seed, part) draws one part's arguments, and reference() takes and returns one part's arrays. A program takes and returns all parts, laid end to end along the dimension named above; each array names one. Nothing has to cross between parts.
Inputs may be any that keep to these rules, and one draw needn't show every extreme that they name: `amp_tiles`: the 4 tiles of one row tile are distinct. Among the 4 row tiles of one pair index no virtual-pair tile is named more than 2 times, and in every draw some tile is named exactly 2 times by the row tiles of some pair index. `int_tiles`: the 2 tiles of one row are distinct, and every virtual-pair tile is named by some row.
All inputs are finite; a program needn't handle non-finite values.
Results may differ from the reference program's by a relative error of at most 0.0049.
Values may be sent and summed in bfloat16 or wider, within the bound.
A program may use at most 128 MiB of HBM per device.

```python
import math
import jax
import jax.numpy as jnp
import numpy as np
from jax import lax

PT = 4096
ROWT = 32
OT_DEV = 4
ROW_TILES = 32
K_T = 4
NP = 8
K_V = 2
CAP = 2


def shard_levels(stream_key, dims, pieces, smallest, largest):
    factor_of, own = 1.0, jax.random.fold_in(stream_key, 6)
    for axis_at, parts in pieces:
        draws = jnp.exp(jax.random.uniform(jax.random.fold_in(own, axis_at), (parts,), jnp.float32, smallest / len(pieces), largest / len(pieces)))
        factor_of = factor_of * jnp.repeat(draws, dims[axis_at] // parts).reshape([-1 if axis == axis_at else 1 for axis in range(len(dims))])
    return factor_of


def choose_distinct(key, rows, count, top, lift):
    sequence = jax.random.permutation(jax.random.fold_in(key, 1), count)
    favour = sequence
    for power in range(3):
        favour = favour * favour // count
    favour = favour * lift // count
    chance = jax.random.randint(jax.random.fold_in(key, 2), (rows, count), 0, 4096) + favour
    holders = jax.random.permutation(jax.random.fold_in(key, 3), rows)[jnp.arange(count) % rows]
    chance = jnp.where(jnp.arange(rows)[:, None] == holders[None, :], 1 << 14, chance)
    priority = chance * count + jnp.arange(count)
    return lax.top_k(priority.astype(jnp.int32), top)[1].astype(jnp.int32)


def assign_block(key, own, number, rows, count, top, reach, slope):
    order = jax.random.permutation(key, count)
    crowded, ordinary = portions_of(count, rows * top, reach, slope, True), portions_of(count, rows * top, reach, slope, False)
    places = jnp.arange(count)

    def named(tallies, rotation):
        used = int((tallies > 0).sum())
        fixed = max(1, used // 4)
        shifted = fixed + (places - fixed + rotation * (used - fixed)) % max(1, count - fixed)
        return jnp.zeros((count,), jnp.int32).at[order[jnp.where(places < fixed, places, shifted)]].set(jnp.asarray(tallies, jnp.int32))

    tallies = jnp.where(number % 4 == 0, named(crowded, number // 4), named(ordinary, number - number // 4 - 1))
    mixed = jax.random.permutation(jax.random.fold_in(own, 3), count)
    giver, receiver = mixed[0:count // 2 * 2:2], mixed[1:count // 2 * 2:2]
    room = jnp.minimum(tallies[giver] - 1, reach - tallies[receiver]) // 2
    room = jnp.where((giver == order[0]) | (receiver == order[0]) | (tallies[receiver] == 0), 0, jnp.maximum(room, 0))
    shifted = jax.random.randint(jax.random.fold_in(own, 4), (count // 2,), 0, 1 << 20) % (room + 1)
    tallies = tallies.at[giver].add(-shifted).at[receiver].add(shifted)
    members = jnp.searchsorted(jnp.cumsum(tallies), jnp.arange(rows * top), side="right").astype(jnp.int32)
    grid = members.reshape(top, rows).T
    grid = grid[jax.random.permutation(jax.random.fold_in(own, 1), rows)]
    rotation = jax.random.randint(jax.random.fold_in(own, 2), (rows, 1), 0, top)
    return jnp.take_along_axis(grid, (jnp.arange(top)[None, :] + rotation) % top, axis=1)


def portions_of(amount, total, limit, lean, full):
    weights = [(1 << 20) // math.isqrt(grade ** lean) + 1 for grade in range(1, amount + 1)]
    largest = limit if full else min(limit, max(-(-total // amount), total * weights[0] // sum(weights)))
    least = 1 if total - largest >= amount - 1 else 0
    counts, surplus = [largest] + [least] * (amount - 1), total - largest - least * (amount - 1)
    while surplus > 0:
        movable = [i for i in range(1, amount) if counts[i] < largest] or [i for i in range(1, amount) if counts[i] < limit]
        mass, remaining = sum([weights[i] for i in movable]), surplus
        for i in movable:
            more = min(limit - counts[i], max(1, remaining * weights[i] // mass), surplus)
            counts[i] = counts[i] + more
            surplus = surplus - more
    return np.array(counts)


def gaussian(own_key, dims, deviation, limit, pieces=(), kind=jnp.bfloat16):
    array = jax.random.normal(own_key, dims, jnp.float32) * deviation
    if len(pieces) > 0:
        array = shard_levels(own_key, dims, pieces, -0.22, 0.18) * array
    return jnp.clip(array, min=-limit, max=limit).astype(kind)


def setup_inputs(seed: int = 0, part: int = 0) -> dict:
    keys = jax.random.split(jax.random.key(seed), 7)
    own_keys = jax.random.split(jax.random.fold_in(keys[6], part), 7)
    amplitudes = gaussian(own_keys[0], (ROW_TILES, K_T, ROWT, PT), 1.0, 6.0, ((0, 8), (2, 2)))
    amp_tiles_keys = jax.random.split(jax.random.fold_in(own_keys[1], 1), ROW_TILES // OT_DEV)
    amp_tiles_turns = jax.random.permutation(jax.random.fold_in(own_keys[1], 3), ROW_TILES // OT_DEV)
    amp_tiles = jax.vmap(lambda own, number: assign_block(jax.random.fold_in(own_keys[1], 2), own, number, OT_DEV, NP, K_T, CAP, 2))(amp_tiles_keys, amp_tiles_turns).reshape((ROW_TILES, K_T))
    integrals = gaussian(own_keys[2], (NP, PT, K_V, PT), PT ** -0.5, 0.09375, ((0, 8), (3, 2)))
    int_tiles = choose_distinct(own_keys[3], NP, NP, K_V, 0)
    occupied_energy = jnp.clip(-3.0 + 2.5 * jax.random.uniform(own_keys[4], (ROW_TILES, ROWT), jnp.float32) ** shard_levels(own_keys[4], (ROW_TILES, ROWT), ((0, 8),), -0.2, 0.2), -3.0, -0.5)
    virtual_energy = jnp.clip(0.5 + 5.5 * jax.random.uniform(own_keys[5], (NP, PT), jnp.float32) ** shard_levels(own_keys[5], (NP, PT), ((1, 2),), -0.2, 0.2), 0.5, 6.0)
    return dict(amplitudes=amplitudes, amp_tiles=amp_tiles, integrals=integrals, int_tiles=int_tiles, occupied_energy=occupied_energy, virtual_energy=virtual_energy)


def reference(amplitudes, amp_tiles, integrals, int_tiles, occupied_energy, virtual_energy):
    tile_total = virtual_energy.shape[0]
    row_total = amplitudes.shape[0]
    flat_amps = amplitudes.reshape(row_total * K_T, ROWT, PT)
    flat_tiles = amp_tiles.reshape(-1).astype(jnp.int32)

    def one_slot(inputs):
        slot_amps, slot_tile = inputs
        slab_cols = lax.dynamic_index_in_dim(integrals, slot_tile, 0, keepdims=False).reshape(PT, K_V * PT)
        return jnp.dot(slot_amps, slab_cols, preferred_element_type=jnp.float32).astype(jnp.bfloat16)

    products = lax.map(one_slot, (flat_amps, flat_tiles)).reshape(row_total, K_T, ROWT, K_V, PT)

    def row_block(inputs):
        block_products, block_tiles, block_energy = inputs
        landing = int_tiles[block_tiles.astype(jnp.int32)].reshape(-1).astype(jnp.int32)
        terms = jnp.transpose(block_products, (0, 2, 1, 3)).reshape(K_T * K_V, ROWT, PT).astype(jnp.float32)
        residual = jnp.zeros((tile_total, ROWT, PT), jnp.float32).at[landing].add(terms)
        denominator = virtual_energy[:, None, :] - block_energy[None, :, None]
        return (residual / denominator).astype(jnp.bfloat16)

    return lax.map(row_block, (products, amp_tiles, occupied_energy))
```

```python
import functools

import jax
import jax.numpy as jnp
from jax import lax
from jax.experimental import pallas as pl
from jax.experimental.pallas import tpu as pltpu
from jax.sharding import PartitionSpec as P

MESH = pl.DeviceIdType.MESH


def flip(index, mask, size):
    out, bit = 0, 1
    while bit < size:
        out = out + ((index // bit + mask // bit) % 2) * bit
        bit *= 2
    return out


def ladder(pairs, ints, reps, tile, packed, right, returned, left, slab, product,
           slab_sem, own_sem, out_send, out_recv, side_send, side_recv, back_send, back_recv, keep_sem):
    spread = ints * reps
    groups = pairs // 2
    me = lax.axis_index("pair")
    mine = lax.axis_index("int") * reps + lax.axis_index("rep")
    chip = me // 2
    rows = left.shape[1] * left.shape[2]
    width = slab.shape[1]
    chunks = slab_sem.shape[0]
    depth = slab.shape[0] // chunks

    def side(step):
        to = (mine + step) % spread
        return {"int": to // reps, "rep": to % reps}

    def load(i):
        part = pl.ds(i * depth, depth)
        return pltpu.make_async_copy(right.at[part], slab.at[part], slab_sem.at[i])

    def outward(j):
        to = flip(me, j, pairs)
        return pltpu.make_async_remote_copy(
            src_ref=packed.at[to], dst_ref=left.at[me, mine],
            send_sem=out_send.at[j], recv_sem=out_recv.at[j],
            device_id={"pair": to}, device_id_type=MESH)

    def arrived(j):
        came = flip(me, j, pairs)
        return pltpu.make_async_remote_copy(
            src_ref=packed.at[came], dst_ref=left.at[came, mine],
            send_sem=out_send.at[j], recv_sem=out_recv.at[j],
            device_id={"pair": came}, device_id_type=MESH)

    def sideways(j, step):
        at = flip(me, j, pairs)
        return pltpu.make_async_remote_copy(
            src_ref=left.at[at, mine], dst_ref=left.at[at, mine],
            send_sem=side_send.at[j, step - 1], recv_sem=side_recv.at[j, step - 1],
            device_id=side(step), device_id_type=MESH)

    def crossed(j, step):
        at = flip(me, j, pairs)
        came = (mine + spread - step) % spread
        return pltpu.make_async_remote_copy(
            src_ref=left.at[at, came], dst_ref=left.at[at, came],
            send_sem=side_send.at[j, step - 1], recv_sem=side_recv.at[j, step - 1],
            device_id=side(step), device_id_type=MESH)

    def back(j):
        to = flip(me, j, pairs)
        return pltpu.make_async_remote_copy(
            src_ref=product.at[to], dst_ref=returned.at[me],
            send_sem=back_send.at[j], recv_sem=back_recv.at[j],
            device_id={"pair": to}, device_id_type=MESH)

    def home(j):
        came = flip(me, j, pairs)
        return pltpu.make_async_remote_copy(
            src_ref=product.at[came], dst_ref=returned.at[came],
            send_sem=back_send.at[j], recv_sem=back_recv.at[j],
            device_id={"pair": came}, device_id_type=MESH)

    own = pltpu.make_async_copy(packed.at[me], left.at[me, mine], own_sem)
    keep = pltpu.make_async_copy(product.at[me], returned.at[me], keep_sem)

    own.start()
    barrier = pltpu.get_barrier_semaphore()
    for j in range(1, pairs):
        pl.semaphore_signal(barrier, inc=1, device_id={"pair": flip(me, j, pairs)}, device_id_type=MESH)
    for step in range(1, spread):
        pl.semaphore_signal(barrier, inc=1, device_id=side(step), device_id_type=MESH)
    pl.semaphore_wait(barrier, pairs + spread - 2)

    @pl.loop(0, pairs - 1)
    def _(i):
        outward(pairs - 1 - i).start()

    @pl.loop(0, chunks)
    def _(i):
        load(i).start()

    def multiply(group):
        at = flip(chip, group, groups)

        @pl.loop(0, width // tile)
        def _(t):
            cols = pl.ds(pl.multiple_of(t * tile, tile), tile)
            part = left[pl.ds(at * 2, 2)].reshape(2 * rows, left.shape[3])
            total = jnp.dot(part, slab[:, cols], preferred_element_type=jnp.float32)
            product[pl.ds(at * 2, 2), :, cols] = total.astype(jnp.bfloat16).reshape(2, rows, tile)

    own.wait()
    for step in range(1, spread):
        sideways(0, step).start()
    arrived(1).wait_recv()
    for step in range(1, spread):
        sideways(1, step).start()

    @pl.loop(0, chunks)
    def _(i):
        load(i).wait()

    for j in range(2):
        for step in range(1, spread):
            crossed(j, step).wait_recv()
    multiply(0)
    keep.start()
    back(1).start()

    @pl.loop(0, groups - 1)
    def _(i):
        group = groups - 1 - i
        for k in range(2):
            j = group * 2 + 1 - k
            arrived(j).wait_recv()
            for step in range(1, spread):
                sideways(j, step).start()
        for k in range(2):
            j = group * 2 + 1 - k
            for step in range(1, spread):
                crossed(j, step).wait_recv()
        multiply(group)
        for k in range(2):
            back(group * 2 + 1 - k).start()

    keep.wait()

    @pl.loop(0, pairs)
    def _(j):
        for step in range(1, spread):
            sideways(j, step).wait_send()

    @pl.loop(1, pairs)
    def _(j):
        outward(j).wait_send()
        back(j).wait_send()
        home(j).wait_recv()


def shards(ints, reps, amplitudes, amp_tiles, integrals, int_tiles, occupied_energy, virtual_energy):
    pairs = lax.axis_size("pair")
    spread = ints * reps
    tile_total = int_tiles.shape[0]
    row_tiles, slot_count, row_local, pair_width = amplitudes.shape
    couplings = integrals.shape[2]
    col_local = integrals.shape[3]
    width = couplings * col_local
    entries = row_tiles * slot_count
    capacity = max(2, (entries + tile_total - 1) // tile_total)
    flat_tiles = amp_tiles.reshape(-1)
    tile_hits = (flat_tiles[:, None] == jnp.arange(tile_total, dtype=jnp.int32)[None, :]).astype(
        jnp.int32
    )
    slot_rank = jnp.sum(tile_hits * (jnp.cumsum(tile_hits, axis=0) - 1), axis=1)
    slot_index = flat_tiles * capacity + slot_rank
    buffer_slots = tile_total * capacity
    dispatch = (jnp.arange(buffer_slots, dtype=jnp.int32)[:, None] == slot_index[None, :]).astype(
        jnp.bfloat16
    )
    right = integrals.reshape(pair_width, width)
    packed = jnp.dot(
        dispatch,
        amplitudes.reshape(entries, row_local * pair_width),
        preferred_element_type=jnp.float32,
    )
    held = capacity * row_local
    padded = -(-held // 16) * 16
    packed = packed.astype(jnp.bfloat16).reshape(pairs, held, pair_width)
    packed = jnp.pad(packed, ((0, 0), (0, padded - held), (0, 0)))
    rows = spread * padded
    chunks = 4
    dma = pltpu.SemaphoreType.DMA
    returned = pl.pallas_call(
        functools.partial(ladder, pairs, ints, reps, 512),
        out_shape=jax.ShapeDtypeStruct((pairs, rows, width), jnp.bfloat16),
        in_specs=[pl.BlockSpec(memory_space=pl.ANY)] * 2,
        out_specs=pl.BlockSpec(memory_space=pl.ANY),
        scratch_shapes=[
            pltpu.VMEM((pairs, spread, padded, pair_width), jnp.bfloat16),
            pltpu.VMEM((pair_width, width), jnp.bfloat16),
            pltpu.VMEM((pairs, rows, width), jnp.bfloat16),
            dma((chunks,)),
            dma,
            dma((pairs,)),
            dma((pairs,)),
            dma((pairs, spread - 1)),
            dma((pairs, spread - 1)),
            dma((pairs,)),
            dma((pairs,)),
            dma,
        ],
        compiler_params=pltpu.CompilerParams(
            collective_id=0, has_side_effects=True, vmem_limit_bytes=56 << 20
        ),
    )(packed, right)
    returned = returned.reshape(pairs, spread, padded, couplings, col_local)[:, :, :held]
    returned = returned.reshape(pairs, spread, capacity, row_local, couplings, col_local)
    targets = jnp.sum(tile_hits[:, :, None] * int_tiles[None, :, :], axis=1)
    row_owner = jnp.arange(entries, dtype=jnp.int32) // slot_count
    dest_rows = row_owner[:, None] * tile_total + targets
    landing = (
        jnp.arange(row_tiles * tile_total, dtype=jnp.int32)[:, None, None] == dest_rows[None, :, :]
    ).astype(jnp.bfloat16)
    combine = jnp.einsum(
        "qjk,sj->qsk", landing, dispatch, preferred_element_type=jnp.float32
    ).astype(jnp.bfloat16)
    combine = combine.reshape(row_tiles * tile_total, pairs, capacity, couplings)
    residual = jnp.einsum("qdak,dxalkc->qxlc", combine, returned, preferred_element_type=jnp.float32)
    residual = residual.reshape(row_tiles, tile_total, spread * row_local, col_local)
    denominator = virtual_energy[None, :, None, :] - occupied_energy[:, None, :, None]
    return (residual / denominator).astype(jnp.bfloat16)


def solution(mesh):
    placed = (
        P(("mol", "pair"), None, ("int", "rep"), None),
        P(("mol", "pair"), None),
        P(("mol", "pair"), None, None, ("int", "rep")),
        P("mol", None),
        P(("mol", "pair"), None),
        P("mol", ("int", "rep")),
    )
    return jax.shard_map(
        functools.partial(shards, mesh.shape["int"], mesh.shape["rep"]),
        mesh=mesh,
        in_specs=placed,
        out_specs=P(("mol", "pair"), None, None, ("int", "rep")),
        check_vma=False,
    )
```

```python
import functools

import jax
import jax.numpy as jnp
from jax import lax
from jax.experimental import pallas as pl
from jax.experimental.pallas import tpu as pltpu
from jax.sharding import PartitionSpec as P

MESH = pl.DeviceIdType.MESH


def flip(index, mask, size):
    out, bit = 0, 1
    while bit < size:
        out = out + ((index // bit + mask // bit) % 2) * bit
        bit *= 2
    return out


def ladder(pairs, ints, reps, tile, packed, right, returned, left, slab, product,
           slab_sem, own_sem, out_send, out_recv, side_send, side_recv, back_send, back_recv, keep_sem):
    spread = ints * reps
    groups = pairs // 2
    me = lax.axis_index("pair")
    mine = lax.axis_index("int") * reps + lax.axis_index("rep")
    chip = me // 2
    rows = left.shape[1] * left.shape[2]
    width = slab.shape[1]
    chunks = slab_sem.shape[0]
    depth = slab.shape[0] // chunks

    def side(step):
        to = (mine + step) % spread
        return {"int": to // reps, "rep": to % reps}

    def load(i):
        part = pl.ds(i * depth, depth)
        return pltpu.make_async_copy(right.at[part], slab.at[part], slab_sem.at[i])

    def outward(j):
        to = flip(me, j, pairs)
        return pltpu.make_async_remote_copy(
            src_ref=packed.at[to], dst_ref=left.at[me, mine],
            send_sem=out_send.at[j], recv_sem=out_recv.at[j],
            device_id={"pair": to}, device_id_type=MESH)

    def arrived(j):
        came = flip(me, j, pairs)
        return pltpu.make_async_remote_copy(
            src_ref=packed.at[came], dst_ref=left.at[came, mine],
            send_sem=out_send.at[j], recv_sem=out_recv.at[j],
            device_id={"pair": came}, device_id_type=MESH)

    def sideways(j, step):
        at = flip(me, j, pairs)
        return pltpu.make_async_remote_copy(
            src_ref=left.at[at, mine], dst_ref=left.at[at, mine],
            send_sem=side_send.at[j, step - 1], recv_sem=side_recv.at[j, step - 1],
            device_id=side(step), device_id_type=MESH)

    def crossed(j, step):
        at = flip(me, j, pairs)
        came = (mine + spread - step) % spread
        return pltpu.make_async_remote_copy(
            src_ref=left.at[at, came], dst_ref=left.at[at, came],
            send_sem=side_send.at[j, step - 1], recv_sem=side_recv.at[j, step - 1],
            device_id=side(step), device_id_type=MESH)

    def back(j):
        to = flip(me, j, pairs)
        return pltpu.make_async_remote_copy(
            src_ref=product.at[to], dst_ref=returned.at[me],
            send_sem=back_send.at[j], recv_sem=back_recv.at[j],
            device_id={"pair": to}, device_id_type=MESH)

    def home(j):
        came = flip(me, j, pairs)
        return pltpu.make_async_remote_copy(
            src_ref=product.at[came], dst_ref=returned.at[came],
            send_sem=back_send.at[j], recv_sem=back_recv.at[j],
            device_id={"pair": came}, device_id_type=MESH)

    own = pltpu.make_async_copy(packed.at[me], left.at[me, mine], own_sem)
    keep = pltpu.make_async_copy(product.at[me], returned.at[me], keep_sem)

    own.start()
    barrier = pltpu.get_barrier_semaphore()
    for j in range(1, pairs):
        pl.semaphore_signal(barrier, inc=1, device_id={"pair": flip(me, j, pairs)}, device_id_type=MESH)
    for step in range(1, spread):
        pl.semaphore_signal(barrier, inc=1, device_id=side(step), device_id_type=MESH)
    pl.semaphore_wait(barrier, pairs + spread - 2)

    @pl.loop(0, pairs - 1)
    def _(i):
        outward(pairs - 1 - i).start()

    @pl.loop(0, chunks)
    def _(i):
        load(i).start()

    def multiply(group):
        at = flip(chip, group, groups)

        @pl.loop(0, width // tile)
        def _(t):
            cols = pl.ds(pl.multiple_of(t * tile, tile), tile)
            part = left[pl.ds(at * 2, 2)].reshape(2 * rows, left.shape[3])
            total = jnp.dot(part, slab[:, cols], preferred_element_type=jnp.float32)
            product[pl.ds(at * 2, 2), :, cols] = total.astype(jnp.bfloat16).reshape(2, rows, tile)

    own.wait()
    for step in range(1, spread):
        sideways(0, step).start()
    arrived(1).wait_recv()
    for step in range(1, spread):
        sideways(1, step).start()

    @pl.loop(0, chunks)
    def _(i):
        load(i).wait()

    for j in range(2):
        for step in range(1, spread):
            crossed(j, step).wait_recv()
    multiply(0)
    keep.start()
    back(1).start()

    @pl.loop(0, groups - 1)
    def _(i):
        group = groups - 1 - i
        for k in range(2):
            j = group * 2 + 1 - k
            arrived(j).wait_recv()
            for step in range(1, spread):
                sideways(j, step).start()
        for k in range(2):
            j = group * 2 + 1 - k
            for step in range(1, spread):
                crossed(j, step).wait_recv()
        multiply(group)
        for k in range(2):
            back(group * 2 + 1 - k).start()

    keep.wait()

    @pl.loop(0, pairs)
    def _(j):
        for step in range(1, spread):
            sideways(j, step).wait_send()

    @pl.loop(1, pairs)
    def _(j):
        outward(j).wait_send()
        back(j).wait_send()
        home(j).wait_recv()


def pack(entries, capacity, tiles, ranks, amplitudes, packed, sem):
    def move(j):
        return pltpu.make_async_copy(
            amplitudes.at[j], packed.at[tiles[j] * capacity + ranks[j]], sem.at[j]
        )

    for j in range(entries):
        move(j).start()
    for j in range(entries):
        move(j).wait()


def combine(row_tiles, slot_count, couplings, spread, row_local, tiles, ranks, targets, occupied, virtual, *refs):
    parts, out, total = refs[:couplings], refs[couplings], refs[couplings + 1]
    tile_total = out.shape[1]
    total[...] = jnp.zeros_like(total)

    for r in range(row_tiles):
        for k in range(slot_count):
            tile = tiles[r * slot_count + k]
            rank = ranks[r * slot_count + k]
            for m in range(couplings):
                at = targets[tile * couplings + m]
                for x in range(spread):
                    span = pl.ds(x * row_local, row_local)
                    total[r, at, span, :] += parts[m][tile, x, rank].astype(jnp.float32)
        for b in range(tile_total):
            denominator = virtual[b : b + 1, :] - occupied[r]
            out[r, b] = (total[r, b] / denominator).astype(jnp.bfloat16)


def shards(ints, reps, amplitudes, amp_tiles, integrals, int_tiles, occupied_energy, virtual_energy):
    pairs = lax.axis_size("pair")
    spread = ints * reps
    tile_total = int_tiles.shape[0]
    row_tiles, slot_count, row_local, pair_width = amplitudes.shape
    couplings = integrals.shape[2]
    col_local = integrals.shape[3]
    width = couplings * col_local
    entries = row_tiles * slot_count
    capacity = max(2, (entries + tile_total - 1) // tile_total)
    flat_tiles = amp_tiles.reshape(-1)
    tile_hits = (flat_tiles[:, None] == jnp.arange(tile_total, dtype=jnp.int32)[None, :]).astype(
        jnp.int32
    )
    slot_rank = jnp.sum(tile_hits * (jnp.cumsum(tile_hits, axis=0) - 1), axis=1)
    right = integrals.reshape(pair_width, width)
    packed = pl.pallas_call(
        functools.partial(pack, entries, capacity),
        out_shape=jax.ShapeDtypeStruct((tile_total * capacity, row_local, pair_width), jnp.bfloat16),
        in_specs=[pl.BlockSpec(memory_space=pltpu.SMEM)] * 2 + [pl.BlockSpec(memory_space=pl.ANY)],
        out_specs=pl.BlockSpec(memory_space=pl.ANY),
        scratch_shapes=[pltpu.SemaphoreType.DMA((entries,))],
    )(flat_tiles, slot_rank, amplitudes.reshape(entries, row_local, pair_width))
    held = capacity * row_local
    padded = -(-held // 16) * 16
    packed = packed.reshape(pairs, held, pair_width)
    packed = jnp.pad(packed, ((0, 0), (0, padded - held), (0, 0)))
    rows = spread * padded
    chunks = 4
    dma = pltpu.SemaphoreType.DMA
    returned = pl.pallas_call(
        functools.partial(ladder, pairs, ints, reps, 512),
        out_shape=jax.ShapeDtypeStruct((pairs, rows, width), jnp.bfloat16),
        in_specs=[pl.BlockSpec(memory_space=pl.ANY)] * 2,
        out_specs=pl.BlockSpec(memory_space=pl.ANY),
        scratch_shapes=[
            pltpu.VMEM((pairs, spread, padded, pair_width), jnp.bfloat16),
            pltpu.VMEM((pair_width, width), jnp.bfloat16),
            pltpu.VMEM((pairs, rows, width), jnp.bfloat16),
            dma((chunks,)),
            dma,
            dma((pairs,)),
            dma((pairs,)),
            dma((pairs, spread - 1)),
            dma((pairs, spread - 1)),
            dma((pairs,)),
            dma((pairs,)),
            dma,
        ],
        compiler_params=pltpu.CompilerParams(
            collective_id=0, has_side_effects=True, vmem_limit_bytes=56 << 20
        ),
    )(packed, right)
    returned = returned.reshape(pairs, spread, padded, width)[:, :, :held]
    returned = returned.reshape(pairs, spread, capacity, row_local, width)
    block = min(512, col_local)
    steps = col_local // block
    full_rows = spread * row_local

    def columns(m):
        return pl.BlockSpec(
            (pairs, spread, capacity, row_local, block), lambda i, *_: (0, 0, 0, 0, m * steps + i)
        )

    return pl.pallas_call(
        functools.partial(combine, row_tiles, slot_count, couplings, spread, row_local),
        out_shape=jax.ShapeDtypeStruct((row_tiles, tile_total, full_rows, col_local), jnp.bfloat16),
        grid_spec=pltpu.PrefetchScalarGridSpec(
            num_scalar_prefetch=3,
            grid=(steps,),
            in_specs=[
                pl.BlockSpec((row_tiles, full_rows, 1), lambda i, *_: (0, 0, 0)),
                pl.BlockSpec((tile_total, block), lambda i, *_: (0, i)),
            ]
            + [columns(m) for m in range(couplings)],
            out_specs=pl.BlockSpec(
                (row_tiles, tile_total, full_rows, block), lambda i, *_: (0, 0, 0, i)
            ),
            scratch_shapes=[pltpu.VMEM((row_tiles, tile_total, full_rows, block), jnp.float32)],
        ),
        compiler_params=pltpu.CompilerParams(vmem_limit_bytes=32 << 20),
    )(flat_tiles, slot_rank, int_tiles.reshape(-1), occupied_energy[:, :, None], virtual_energy,
      *([returned] * couplings))


def solution(mesh):
    placed = (
        P(("mol", "pair"), None, ("int", "rep"), None),
        P(("mol", "pair"), None),
        P(("mol", "pair"), None, None, ("int", "rep")),
        P("mol", None),
        P(("mol", "pair"), None),
        P("mol", ("int", "rep")),
    )
    return jax.shard_map(
        functools.partial(shards, mesh.shape["int"], mesh.shape["rep"]),
        mesh=mesh,
        in_specs=placed,
        out_specs=P(("mol", "pair"), None, None, ("int", "rep")),
        check_vma=False,
    )
```

```python
import functools

import jax
import jax.numpy as jnp
from jax import lax
from jax.experimental import pallas as pl
from jax.experimental.pallas import tpu as pltpu
from jax.sharding import PartitionSpec as P

MESH = pl.DeviceIdType.MESH


def flip(index, mask, size):
    out, bit = 0, 1
    while bit < size:
        out = out + ((index // bit + mask // bit) % 2) * bit
        bit *= 2
    return out


def ladder(pairs, ints, reps, tile, packed, right, returned, left, slab, product,
           slab_sem, own_sem, out_send, out_recv, side_send, side_recv, back_send, back_recv, keep_sem):
    spread = ints * reps
    groups = pairs // 2
    me = lax.axis_index("pair")
    mine = lax.axis_index("int") * reps + lax.axis_index("rep")
    chip = me // 2
    rows = left.shape[1] * left.shape[2]
    width = slab.shape[1]
    chunks = slab_sem.shape[0]
    depth = slab.shape[0] // chunks

    def side(step):
        to = (mine + step) % spread
        return {"int": to // reps, "rep": to % reps}

    def load(i):
        part = pl.ds(i * depth, depth)
        return pltpu.make_async_copy(right.at[part], slab.at[part], slab_sem.at[i])

    def outward(j):
        to = flip(me, j, pairs)
        return pltpu.make_async_remote_copy(
            src_ref=packed.at[to], dst_ref=left.at[me, mine],
            send_sem=out_send.at[j], recv_sem=out_recv.at[j],
            device_id={"pair": to}, device_id_type=MESH)

    def arrived(j):
        came = flip(me, j, pairs)
        return pltpu.make_async_remote_copy(
            src_ref=packed.at[came], dst_ref=left.at[came, mine],
            send_sem=out_send.at[j], recv_sem=out_recv.at[j],
            device_id={"pair": came}, device_id_type=MESH)

    def sideways(j, step):
        at = flip(me, j, pairs)
        return pltpu.make_async_remote_copy(
            src_ref=left.at[at, mine], dst_ref=left.at[at, mine],
            send_sem=side_send.at[j, step - 1], recv_sem=side_recv.at[j, step - 1],
            device_id=side(step), device_id_type=MESH)

    def crossed(j, step):
        at = flip(me, j, pairs)
        came = (mine + spread - step) % spread
        return pltpu.make_async_remote_copy(
            src_ref=left.at[at, came], dst_ref=left.at[at, came],
            send_sem=side_send.at[j, step - 1], recv_sem=side_recv.at[j, step - 1],
            device_id=side(step), device_id_type=MESH)

    def back(j):
        to = flip(me, j, pairs)
        return pltpu.make_async_remote_copy(
            src_ref=product.at[to], dst_ref=returned.at[me],
            send_sem=back_send.at[j], recv_sem=back_recv.at[j],
            device_id={"pair": to}, device_id_type=MESH)

    def home(j):
        came = flip(me, j, pairs)
        return pltpu.make_async_remote_copy(
            src_ref=product.at[came], dst_ref=returned.at[came],
            send_sem=back_send.at[j], recv_sem=back_recv.at[j],
            device_id={"pair": came}, device_id_type=MESH)

    own = pltpu.make_async_copy(packed.at[me], left.at[me, mine], own_sem)
    keep = pltpu.make_async_copy(product.at[me], returned.at[me], keep_sem)

    own.start()
    barrier = pltpu.get_barrier_semaphore()
    for j in range(1, pairs):
        pl.semaphore_signal(barrier, inc=1, device_id={"pair": flip(me, j, pairs)}, device_id_type=MESH)
    for step in range(1, spread):
        pl.semaphore_signal(barrier, inc=1, device_id=side(step), device_id_type=MESH)
    pl.semaphore_wait(barrier, pairs + spread - 2)

    @pl.loop(0, pairs - 1)
    def _(i):
        outward(pairs - 1 - i).start()

    @pl.loop(0, chunks)
    def _(i):
        load(i).start()

    def multiply(group):
        at = flip(chip, group, groups)

        @pl.loop(0, width // tile)
        def _(t):
            cols = pl.ds(pl.multiple_of(t * tile, tile), tile)
            part = left[pl.ds(at * 2, 2)].reshape(2 * rows, left.shape[3])
            total = jnp.dot(part, slab[:, cols], preferred_element_type=jnp.float32)
            product[pl.ds(at * 2, 2), :, cols] = total.astype(jnp.bfloat16).reshape(2, rows, tile)

    own.wait()
    for step in range(1, spread):
        sideways(0, step).start()
    arrived(1).wait_recv()
    for step in range(1, spread):
        sideways(1, step).start()

    @pl.loop(0, chunks)
    def _(i):
        load(i).wait()

    for j in range(2):
        for step in range(1, spread):
            crossed(j, step).wait_recv()
    multiply(0)
    keep.start()
    back(1).start()

    @pl.loop(0, groups - 1)
    def _(i):
        group = groups - 1 - i
        for k in range(2):
            j = group * 2 + 1 - k
            arrived(j).wait_recv()
            for step in range(1, spread):
                sideways(j, step).start()
        for k in range(2):
            j = group * 2 + 1 - k
            for step in range(1, spread):
                crossed(j, step).wait_recv()
        multiply(group)
        for k in range(2):
            back(group * 2 + 1 - k).start()

    keep.wait()

    @pl.loop(0, pairs)
    def _(j):
        for step in range(1, spread):
            sideways(j, step).wait_send()

    @pl.loop(1, pairs)
    def _(j):
        outward(j).wait_send()
        back(j).wait_send()
        home(j).wait_recv()


def combine(row_tiles, slot_count, couplings, spread, row_local, tiles, ranks, targets, occupied, virtual, *refs):
    parts, out, total = refs[:couplings], refs[couplings], refs[couplings + 1]
    tile_total = out.shape[1]
    total[...] = jnp.zeros_like(total)

    for r in range(row_tiles):
        for k in range(slot_count):
            tile = tiles[r * slot_count + k]
            rank = ranks[r * slot_count + k]
            for m in range(couplings):
                at = targets[tile * couplings + m]
                for x in range(spread):
                    span = pl.ds(x * row_local, row_local)
                    total[r, at, span, :] += parts[m][tile, x, rank].astype(jnp.float32)
        for b in range(tile_total):
            denominator = virtual[b : b + 1, :] - occupied[r]
            out[r, b] = (total[r, b] / denominator).astype(jnp.bfloat16)


def shards(ints, reps, amplitudes, amp_tiles, integrals, int_tiles, occupied_energy, virtual_energy):
    pairs = lax.axis_size("pair")
    spread = ints * reps
    tile_total = int_tiles.shape[0]
    row_tiles, slot_count, row_local, pair_width = amplitudes.shape
    couplings = integrals.shape[2]
    col_local = integrals.shape[3]
    width = couplings * col_local
    entries = row_tiles * slot_count
    capacity = max(2, (entries + tile_total - 1) // tile_total)
    flat_tiles = amp_tiles.reshape(-1)
    tile_hits = (flat_tiles[:, None] == jnp.arange(tile_total, dtype=jnp.int32)[None, :]).astype(
        jnp.int32
    )
    slot_rank = jnp.sum(tile_hits * (jnp.cumsum(tile_hits, axis=0) - 1), axis=1)
    right = integrals.reshape(pair_width, width)
    slot_index = flat_tiles * capacity + slot_rank
    buffer_slots = tile_total * capacity
    dispatch = (jnp.arange(buffer_slots, dtype=jnp.int32)[:, None] == slot_index[None, :]).astype(
        jnp.bfloat16
    )
    packed = jnp.dot(
        dispatch,
        amplitudes.reshape(entries, row_local * pair_width),
        preferred_element_type=jnp.float32,
    ).astype(jnp.bfloat16)
    held = capacity * row_local
    padded = -(-held // 16) * 16
    packed = packed.reshape(pairs, held, pair_width)
    packed = jnp.pad(packed, ((0, 0), (0, padded - held), (0, 0)))
    rows = spread * padded
    chunks = 4
    dma = pltpu.SemaphoreType.DMA
    returned = pl.pallas_call(
        functools.partial(ladder, pairs, ints, reps, 512),
        out_shape=jax.ShapeDtypeStruct((pairs, rows, width), jnp.bfloat16),
        in_specs=[pl.BlockSpec(memory_space=pl.ANY)] * 2,
        out_specs=pl.BlockSpec(memory_space=pl.ANY),
        scratch_shapes=[
            pltpu.VMEM((pairs, spread, padded, pair_width), jnp.bfloat16),
            pltpu.VMEM((pair_width, width), jnp.bfloat16),
            pltpu.VMEM((pairs, rows, width), jnp.bfloat16),
            dma((chunks,)),
            dma,
            dma((pairs,)),
            dma((pairs,)),
            dma((pairs, spread - 1)),
            dma((pairs, spread - 1)),
            dma((pairs,)),
            dma((pairs,)),
            dma,
        ],
        compiler_params=pltpu.CompilerParams(
            collective_id=0, has_side_effects=True, vmem_limit_bytes=56 << 20
        ),
    )(packed, right)
    returned = returned.reshape(pairs, spread, padded, width)[:, :, :held]
    returned = returned.reshape(pairs, spread, capacity, row_local, width)
    block = min(512, col_local)
    steps = col_local // block
    full_rows = spread * row_local

    def columns(m):
        return pl.BlockSpec(
            (pairs, spread, capacity, row_local, block), lambda i, *_: (0, 0, 0, 0, m * steps + i)
        )

    return pl.pallas_call(
        functools.partial(combine, row_tiles, slot_count, couplings, spread, row_local),
        out_shape=jax.ShapeDtypeStruct((row_tiles, tile_total, full_rows, col_local), jnp.bfloat16),
        grid_spec=pltpu.PrefetchScalarGridSpec(
            num_scalar_prefetch=3,
            grid=(steps,),
            in_specs=[
                pl.BlockSpec((row_tiles, full_rows, 1), lambda i, *_: (0, 0, 0)),
                pl.BlockSpec((tile_total, block), lambda i, *_: (0, i)),
            ]
            + [columns(m) for m in range(couplings)],
            out_specs=pl.BlockSpec(
                (row_tiles, tile_total, full_rows, block), lambda i, *_: (0, 0, 0, i)
            ),
            scratch_shapes=[pltpu.VMEM((row_tiles, tile_total, full_rows, block), jnp.float32)],
        ),
        compiler_params=pltpu.CompilerParams(vmem_limit_bytes=32 << 20),
    )(flat_tiles, slot_rank, int_tiles.reshape(-1), occupied_energy[:, :, None], virtual_energy,
      *([returned] * couplings))


def solution(mesh):
    placed = (
        P(("mol", "pair"), None, ("int", "rep"), None),
        P(("mol", "pair"), None),
        P(("mol", "pair"), None, None, ("int", "rep")),
        P("mol", None),
        P(("mol", "pair"), None),
        P("mol", ("int", "rep")),
    )
    return jax.shard_map(
        functools.partial(shards, mesh.shape["int"], mesh.shape["rep"]),
        mesh=mesh,
        in_specs=placed,
        out_specs=P(("mol", "pair"), None, None, ("int", "rep")),
        check_vma=False,
    )
```
